32 devices in a mesh: groups: 2 (over x), pool: 8 (over z, y), tensor: 2 (over core).
Axes of the slice: x: 2, y: 2, z: 4, core: 2. Of those that a mesh axis runs over, the one named last changes fastest.
Arguments:
- hidden: bfloat16 [16384, 8192], P(('groups', 'pool'), 'tensor'), parts along dimension 0, may hold values from -300 to 300
- norm_gain: bfloat16 [8192], P('tensor'), may hold values from 0.099609375 to 1.8984375
- key_value_weight: bfloat16 [8192, 2, 512], P('tensor', None, 'pool'), may hold values from -0.0625 to 0.0625
- key_value_bias: bfloat16 [2, 512], P(None, 'tensor'), may hold values from -3 to 3
- stored_page_pool: bfloat16 [64, 128, 2, 512], P(('groups', 'pool'), None, None, 'tensor'), parts along dimension 0, may hold values from -6 to 6
- page_request: int32 [64], P(('groups', 'pool')), parts along dimension 0, may hold values from 0 to 7, as said below
- prefix_len: int32 [16], P(('groups', 'pool')), parts along dimension 0, may hold values from 1 to 1024, as said below
- queries: bfloat16 [512, 4096], P(('groups', 'pool'), 'tensor'), parts along dimension 0, may hold values from -20 to 20
- new_key_value: bfloat16 [512, 2, 512], P(('groups', 'pool'), None, 'tensor'), parts along dimension 0, may hold values from -6 to 6
Outputs:
- attended: bfloat16 [512, 4096], P(('groups', 'pool'), 'tensor'), parts along dimension 0
The draws below stay inside these ranges and needn't reach their ends.
There are 2 independent parts, one for each index of `groups`. The reference program is written for one: setup_inputs(seed, part) draws one part's arguments, and reference() takes and returns one part's arrays. A program takes and returns all parts, laid end to end along the dimension named above; an argument that names none is the same for every part. Nothing has to cross between parts.
Inputs may be any that keep to these rules, and one draw needn't show every extreme that they name: `page_request`: each device's 4 pages name requests of the group; no device stores more than 1 pages of one request; in every draw one request has exactly 1 pages on every device. `prefix_len`: some request has the whole 1024 rows.
All inputs are finite; a program needn't handle non-finite values.
Results may differ from the reference program's by a relative error of at most 0.015.
Values may be sent and summed in bfloat16 or wider, within the bound.
A program may use at most 128 MiB of HBM per device.

```python
import math
import jax
import jax.numpy as jnp
from jax import lax

MODEL_WIDTH = 8192
KEY_HEADS = 4
HEADS_PER_GROUP = 8
HEAD_WIDTH = 128
PAGE_TOKENS = 128
CAP = 1
HIDDEN_ROWS = 1024
NEW_TOKENS = 32
REQUEST_COUNT = 8
PAGES = 4
STORED_PAGES = 32
N_POOL = 8


def shared_keys(key):
    row_weight_total = REQUEST_COUNT * NEW_TOKENS
    unrotated_keys = jnp.clip(jax.random.normal(jax.random.fold_in(key, 101), (row_weight_total, KEY_HEADS, HEAD_WIDTH), jnp.float32), -6.0, 6.0)
    return unrotated_keys


def rising_columns(key, top_scale):
    ramp = jnp.arange(MODEL_WIDTH, dtype=jnp.float32) / MODEL_WIDTH
    base_part = jnp.exp(math.log(0.5) + ramp * math.log(top_scale / 0.5))
    jitter = jnp.exp(jax.random.uniform(key, (MODEL_WIDTH,), jnp.float32, 0.0, math.log(2.0)))
    return (base_part * jitter)[None, :]


def draw_hidden(key, part):
    key = jax.random.fold_in(key, 1)
    key_one, key_two, key_three = jax.random.split(key, 3)
    row_weight_total = REQUEST_COUNT * HIDDEN_ROWS
    sampled_inputs = jnp.clip(jax.random.normal(key_one, (row_weight_total, MODEL_WIDTH), jnp.float32), -6.0, 6.0)
    row_scale = jnp.exp(jax.random.uniform(key_two, (row_weight_total, 1), jnp.float32, 0.0, math.log(10.0)))
    column_scale = rising_columns(key_three, 2.5)
    return (sampled_inputs * row_scale * column_scale).astype(jnp.bfloat16)


def draw_prefix_len(key, part):
    key = jax.random.fold_in(key, 3)
    key_one, key_two = jax.random.split(key)
    lengths = jax.random.randint(key_one, (REQUEST_COUNT,), 1, HIDDEN_ROWS + 1)
    longest = jax.random.randint(key_two, (), 0, REQUEST_COUNT)
    return jnp.where(jnp.arange(REQUEST_COUNT) == longest, HIDDEN_ROWS, lengths).astype(jnp.int32)


def draw_page_request(key, part):
    key = jax.random.fold_in(key, 5)
    key_one, key_two, key_three, key_four = jax.random.split(key, 4)
    chosen = PAGES // CAP
    busy_request = jax.random.randint(key_one, (), 0, N_POOL)
    popular = jax.random.randint(key_two, (N_POOL,), 0, 4)
    noise = jax.random.randint(key_three, (N_POOL, N_POOL), 0, 8)
    column = jnp.arange(N_POOL, dtype=jnp.int32)
    scores = (popular[None, :] * 8 + noise) * N_POOL + column[None, :]
    scores = jnp.where(column[None, :] == busy_request, -1, scores)
    others = lax.top_k(scores, chosen - 1)[1].astype(jnp.int32)
    named = jnp.concatenate([jnp.full((N_POOL, 1), busy_request, jnp.int32), others], axis=1)
    named = jnp.repeat(named, CAP, axis=1)
    order_keys = jax.random.randint(key_four, (N_POOL, PAGES), 0, 1 << 20) * PAGES + jnp.arange(PAGES, dtype=jnp.int32)[None, :]
    shuffle = jnp.argsort(order_keys, axis=1)
    return jnp.take_along_axis(named, shuffle, axis=1).reshape(STORED_PAGES).astype(jnp.int32)


def draw_new_key_value(key, part):
    unrotated_keys = shared_keys(key)
    key = jax.random.fold_in(key, 7)
    row_weight_total = REQUEST_COUNT * NEW_TOKENS
    value_rows = jnp.clip(jax.random.normal(key, (row_weight_total, KEY_HEADS, HEAD_WIDTH), jnp.float32), -6.0, 6.0)
    key_portion = unrotated_keys
    return jnp.stack([key_portion, value_rows], axis=1).reshape(row_weight_total, 2, KEY_HEADS * HEAD_WIDTH).astype(jnp.bfloat16)


def draw_queries(key, part):
    key = jax.random.fold_in(key, 9)
    row_weight_total = REQUEST_COUNT * NEW_TOKENS
    query_shape = (row_weight_total, KEY_HEADS, HEADS_PER_GROUP, HEAD_WIDTH)
    sampled_inputs = jnp.clip(2.5 * jax.random.normal(key, query_shape, jnp.float32), -15.0, 15.0)
    return sampled_inputs.reshape(row_weight_total, KEY_HEADS * HEADS_PER_GROUP * HEAD_WIDTH).astype(jnp.bfloat16)


def block_scale(own_key, extent, pieces, smallest, high):
    level = 1.0
    for axis_at, blocks in pieces:
        draws = jax.random.uniform(jax.random.fold_in(jax.random.fold_in(own_key, 6), axis_at), (blocks,), jnp.float32, smallest / len(pieces), high / len(pieces))
        level = level * jnp.repeat(jnp.exp(draws), extent[axis_at] // blocks).reshape((-1,) + (1,) * (len(extent) - 1 - axis_at))
    return level


def bell_draw(rng, dims, spread, bound, pieces=(), held_as=jnp.bfloat16):
    entries = jax.random.normal(rng, dims, jnp.float32) * spread
    if len(pieces) > 0:
        entries = block_scale(rng, dims, pieces, -0.22, 0.18) * entries
    return jnp.clip(entries, min=-bound, max=bound).astype(held_as)


def setup_inputs(seed: int = 0, part: int = 0) -> dict:
    streams_of = jax.random.split(jax.random.key(seed), 10)
    part_splits = jax.random.split(jax.random.fold_in(streams_of[9], part), 10)
    hidden = draw_hidden(jax.random.fold_in(jax.random.fold_in(streams_of[9], part), 71), part)
    norm_gain = jnp.clip(1.0 + 0.18 * jax.random.normal(streams_of[1], (MODEL_WIDTH,), jnp.float32), 0.099609375, 1.8984375).astype(jnp.bfloat16)
    key_value_weight = bell_draw(streams_of[2], (MODEL_WIDTH, 2, KEY_HEADS * HEAD_WIDTH), MODEL_WIDTH ** -0.5, 0.0625, ((0, 2), (2, 8)))
    key_value_bias = bell_draw(streams_of[3], (2, KEY_HEADS * HEAD_WIDTH), 0.5, 3.0, ((1, 2),))
    stored_page_pool = bell_draw(part_splits[4], (STORED_PAGES, PAGE_TOKENS, 2, KEY_HEADS * HEAD_WIDTH), 1.0, 6.0, ((0, 8), (3, 2)))
    page_request = draw_page_request(jax.random.fold_in(jax.random.fold_in(streams_of[9], part), 71), part)
    prefix_len = draw_prefix_len(jax.random.fold_in(jax.random.fold_in(streams_of[9], part), 71), part)
    queries = draw_queries(jax.random.fold_in(jax.random.fold_in(streams_of[9], part), 71), part)
    new_key_value = draw_new_key_value(jax.random.fold_in(jax.random.fold_in(streams_of[9], part), 71), part)
    return dict(hidden=hidden, norm_gain=norm_gain, key_value_weight=key_value_weight, key_value_bias=key_value_bias, stored_page_pool=stored_page_pool, page_request=page_request, prefix_len=prefix_len, queries=queries, new_key_value=new_key_value)


rope_base = 1000000.0
epsilon = 1e-06

def apply_rotation(key_portion, token_positions):
    half_dim = key_portion.shape[-1] // 2
    frequency = rope_base ** (-(jnp.arange(half_dim, dtype=jnp.float32) * 2.0 / key_portion.shape[-1]))
    angles = token_positions.astype(jnp.float32)[:, None] * frequency[None, :]
    cosine = jnp.cos(angles)[:, None, :]
    sine_part = jnp.sin(angles)[:, None, :]
    lead_half = key_portion[..., :half_dim]
    tail_half = key_portion[..., half_dim:]
    return jnp.concatenate([lead_half * cosine - tail_half * sine_part, tail_half * cosine + lead_half * sine_part], axis=-1)

def reference(hidden, norm_gain, key_value_weight, key_value_bias, stored_page_pool, page_request, prefix_len, queries, new_key_value):
    wide_hidden = hidden.astype(jnp.float32)
    scaled_scores = (wide_hidden * norm_gain.astype(jnp.float32)[None, :]).astype(jnp.bfloat16)
    inverse_frequency = lax.rsqrt(lax.optimization_barrier(jnp.mean(wide_hidden * wide_hidden, axis=1)) + epsilon)
    projected_hidden = jnp.dot(scaled_scores, key_value_weight.reshape(MODEL_WIDTH, 2 * KEY_HEADS * HEAD_WIDTH), preferred_element_type=jnp.float32).reshape(-1, 2, KEY_HEADS, HEAD_WIDTH)
    projected_hidden = inverse_frequency[:, None, None, None] * projected_hidden + key_value_bias.astype(jnp.float32).reshape(1, 2, KEY_HEADS, HEAD_WIDTH)
    token_positions = jnp.tile(jnp.arange(HIDDEN_ROWS, dtype=jnp.int32), REQUEST_COUNT)
    restored_prefix_keys = apply_rotation(projected_hidden[:, 0], token_positions).astype(jnp.bfloat16).reshape(REQUEST_COUNT, HIDDEN_ROWS, KEY_HEADS, HEAD_WIDTH)
    restored_prefix_values = projected_hidden[:, 1].astype(jnp.bfloat16).reshape(REQUEST_COUNT, HIDDEN_ROWS, KEY_HEADS, HEAD_WIDTH)
    stored_entries = stored_page_pool.reshape(STORED_PAGES, PAGE_TOKENS, 2, KEY_HEADS, HEAD_WIDTH)
    newest_tokens = new_key_value.reshape(REQUEST_COUNT, NEW_TOKENS, 2, KEY_HEADS, HEAD_WIDTH)
    query_matrix_rows = queries.reshape(REQUEST_COUNT, NEW_TOKENS, KEY_HEADS, HEADS_PER_GROUP, HEAD_WIDTH)
    slot_total_count = N_POOL * CAP
    store_order = jnp.arange(STORED_PAGES, dtype=jnp.int32)
    causal = jnp.arange(NEW_TOKENS, dtype=jnp.int32)[None, :] <= jnp.arange(NEW_TOKENS, dtype=jnp.int32)[:, None]

    def restore_one(request):
        belongs = page_request == request
        unused, selected_pages = lax.top_k(jnp.where(belongs, STORED_PAGES - store_order, -1), slot_total_count)
        is_live = belongs[selected_pages]
        page_token_rows = stored_entries[selected_pages].reshape(slot_total_count * PAGE_TOKENS, 2, KEY_HEADS, HEAD_WIDTH)
        context_keys = jnp.concatenate([restored_prefix_keys[request], page_token_rows[:, 0], newest_tokens[request][:, 0]], axis=0)
        context_values = jnp.concatenate([restored_prefix_values[request], page_token_rows[:, 1], newest_tokens[request][:, 1]], axis=0)
        context_keys = lax.optimization_barrier(context_keys)
        context_values = lax.optimization_barrier(context_values)
        prefix_ok = jnp.arange(HIDDEN_ROWS, dtype=jnp.int32) < prefix_len[request]
        earlier_ok = jnp.concatenate([prefix_ok, jnp.repeat(is_live, PAGE_TOKENS)], axis=0)
        visible = jnp.concatenate([jnp.broadcast_to(earlier_ok[None, :], (NEW_TOKENS, earlier_ok.shape[0])), causal], axis=1)
        query_part = query_matrix_rows[request].astype(jnp.float32)
        scores = jnp.einsum('qhgd,khd->hgqk', query_part, context_keys.astype(jnp.float32)) * HEAD_WIDTH ** (-0.5)
        scores = jnp.where(visible[None, None], scores, -jnp.inf)
        highest = lax.optimization_barrier(jnp.max(scores, axis=-1, keepdims=True))
        exponent = jnp.exp(scores - highest)
        denominator = lax.optimization_barrier(jnp.sum(exponent, axis=-1))
        weights = lax.optimization_barrier(exponent.astype(jnp.bfloat16))
        summed = jnp.einsum('hgqk,khd->qhgd', weights.astype(jnp.float32), context_values.astype(jnp.float32))
        attention_output_rows = summed / jnp.transpose(denominator, (2, 0, 1))[..., None]
        return attention_output_rows.reshape(NEW_TOKENS, KEY_HEADS * HEADS_PER_GROUP * HEAD_WIDTH).astype(jnp.bfloat16)
    attended = lax.map(restore_one, jnp.arange(REQUEST_COUNT, dtype=jnp.int32))
    return attended.reshape(REQUEST_COUNT * NEW_TOKENS, KEY_HEADS * HEADS_PER_GROUP * HEAD_WIDTH)
```

```python
import math

import numpy as np
import jax
import jax.numpy as jnp
from jax import lax
from jax.experimental import pallas as pl
from jax.experimental.pallas import tpu as pltpu
from jax.sharding import PartitionSpec as P

MODEL_WIDTH = 8192
HEADS_PER_GROUP = 8
HEAD_WIDTH = 128
CAP = 1


rope_base = 1000000.0
epsilon = 1e-06
MESH = pl.DeviceIdType.MESH


def apply_rotation(key_portion, token_positions):
    half_dim = key_portion.shape[-1] // 2
    frequency = rope_base ** (
        -(jnp.arange(half_dim, dtype=jnp.float32) * 2.0 / key_portion.shape[-1])
    )
    angles = token_positions.astype(jnp.float32)[:, None] * frequency[None, :]
    cosine = jnp.cos(angles)[:, None, :]
    sine_part = jnp.sin(angles)[:, None, :]
    lead_half = key_portion[..., :half_dim]
    tail_half = key_portion[..., half_dim:]
    return jnp.concatenate(
        [lead_half * cosine - tail_half * sine_part, tail_half * cosine + lead_half * sine_part],
        axis=-1,
    )


def absorb(running, query_heads, key_portion, value_part, visible):
    highest, mass_sum, weighted = running
    scores = jnp.einsum(
        "hgqd,khd->hgqk", query_heads, key_portion, preferred_element_type=jnp.float32
    ) * query_heads.shape[-1] ** (-0.5)
    scores = jnp.where(visible, scores, -jnp.inf)
    new_high = jnp.maximum(highest, jnp.max(scores, axis=-1))
    anchor = jnp.where(jnp.isfinite(new_high), new_high, 0.0)
    prob_rows = jnp.exp(scores - anchor[..., None])
    factor = jnp.exp(highest - anchor)
    mass_sum = mass_sum * factor + jnp.sum(prob_rows, axis=-1)
    weighted = weighted * factor[..., None] + jnp.einsum(
        "hgqk,khd->hgqd",
        prob_rows.astype(jnp.bfloat16),
        value_part,
        preferred_element_type=jnp.float32,
    )
    return (new_high, mass_sum, weighted)


def local(
    hidden,
    norm_gain,
    key_value_weight,
    key_value_bias,
    stored_page_pool,
    page_request,
    prefix_len,
    queries,
    new_key_value,
):
    row_count = hidden.shape[0]
    wide_hidden = hidden.astype(jnp.float32)
    scaled_scores = (wide_hidden * norm_gain.astype(jnp.float32)[None, :]).astype(jnp.bfloat16)
    local_squares = jnp.sum(wide_hidden * wide_hidden, axis=1)
    piece = lax.all_gather(key_value_weight, "pool", axis=2, tiled=True)
    width_part = piece.shape[2]
    product = jnp.dot(
        scaled_scores,
        piece.reshape(piece.shape[0], 2 * width_part),
        preferred_element_type=jnp.float32,
    )
    partial_value = product.reshape(row_count, 2, width_part)
    squares = lax.psum(local_squares, "tensor")
    projected_hidden = lax.psum_scatter(
        partial_value.astype(jnp.bfloat16), "tensor", scatter_dimension=2, tiled=True
    ).astype(jnp.float32)
    inverse_frequency = lax.rsqrt(squares / MODEL_WIDTH + epsilon)
    local_heads = projected_hidden.shape[2] // HEAD_WIDTH
    kv_rows = (
        inverse_frequency[:, None, None] * projected_hidden
        + key_value_bias.astype(jnp.float32)[None]
    )
    kv_rows = kv_rows.reshape(row_count, 2, local_heads, HEAD_WIDTH)
    token_positions = jnp.arange(row_count, dtype=jnp.int32)
    restored_prefix_keys = apply_rotation(kv_rows[:, 0], token_positions).astype(jnp.bfloat16)
    restored_prefix_values = kv_rows[:, 1].astype(jnp.bfloat16)
    fresh_count = queries.shape[0]
    query_heads = queries.reshape(fresh_count, local_heads, HEADS_PER_GROUP, HEAD_WIDTH).transpose(
        1, 2, 0, 3
    )
    fresh_keys = new_key_value[:, 0].reshape(fresh_count, local_heads, HEAD_WIDTH)
    fresh_values = new_key_value[:, 1].reshape(fresh_count, local_heads, HEAD_WIDTH)
    prefix_ok = token_positions < prefix_len[0]
    causal = jnp.arange(fresh_count)[None, :] <= jnp.arange(fresh_count)[:, None]
    visible = jnp.concatenate(
        [jnp.broadcast_to(prefix_ok[None, :], (fresh_count, row_count)), causal], axis=1
    )
    start_state = (
        jnp.full((local_heads, HEADS_PER_GROUP, fresh_count), -jnp.inf, jnp.float32),
        jnp.zeros((local_heads, HEADS_PER_GROUP, fresh_count), jnp.float32),
        jnp.zeros((local_heads, HEADS_PER_GROUP, fresh_count, HEAD_WIDTH), jnp.float32),
    )
    running = absorb(
        start_state,
        query_heads,
        jnp.concatenate([restored_prefix_keys, fresh_keys], axis=0),
        jnp.concatenate([restored_prefix_values, fresh_values], axis=0),
        visible,
    )
    page_count = page_request.shape[0]
    page_index = jnp.arange(page_count)
    same_request = (page_request[:, None] == page_request[None, :]) & (
        page_index[None, :] < page_index[:, None]
    )
    slot_rank = jnp.sum(same_request.astype(jnp.int32), axis=1)
    pool_size = lax.axis_size("pool")
    page_len = stored_page_pool.shape[1]
    outgoing = (
        jnp.zeros((pool_size, CAP) + stored_page_pool.shape[1:], jnp.bfloat16)
        .at[page_request, slot_rank]
        .set(stored_page_pool)
    )
    occupied = jnp.zeros((pool_size, CAP), jnp.bfloat16).at[page_request, slot_rank].set(1.0)
    arrived, present = (
        lax.all_to_all(outgoing, "pool", split_axis=0, concat_axis=0, tiled=True),
        lax.all_to_all(occupied, "pool", split_axis=0, concat_axis=0, tiled=True),
    )
    slot_total_count = pool_size * CAP
    per_block = math.gcd(slot_total_count, max(1, 1024 // page_len))
    grouped = arrived.reshape(
        slot_total_count // per_block, per_block * page_len, 2, local_heads, HEAD_WIDTH
    )
    live_keys = (
        jnp.repeat(present.reshape(slot_total_count // per_block, per_block), page_len, axis=1)
        > 0.5
    )

    def visit_block(carried, scan_item):
        page_block, is_live = scan_item
        return (
            absorb(carried, query_heads, page_block[:, 0], page_block[:, 1], is_live[None, :]),
            None,
        )

    running, unused = lax.scan(visit_block, running, (grouped, live_keys))
    highest, mass_sum, weighted = running
    attended = weighted / mass_sum[..., None]
    return attended.transpose(2, 0, 1, 3).reshape(fresh_count, -1).astype(jnp.bfloat16)


NSUB = 2
MASKED = -1e30
FLAG_ROWS = 16


def rotation_tables(row_count):
    half = HEAD_WIDTH // 2
    frequency = rope_base ** (-(np.arange(half, dtype=np.float64) * 2.0 / HEAD_WIDTH))
    angles = np.arange(row_count, dtype=np.float64)[:, None] * frequency[None, :]
    cosine, sine = np.cos(angles), np.sin(angles)
    return (
        np.concatenate([cosine, cosine], axis=1).astype(np.float32),
        np.concatenate([-sine, sine], axis=1).astype(np.float32),
    )


def fused_kernel(
    w_ref, h_ref, gain_ref, bias_ref, page_ref, req_ref, plen_ref, q_ref, nkv_ref, cos_ref, sin_ref,
    out_ref,
    wbuf, hraw, hs, accs, psend_buf, precv_buf, ss_send, ss_recv, pout, pin, qbuf, kbuf, vbuf, obuf,
    m_st, l_st, a_st,
    h_sem, own_sem, page_self_sem, w_send, w_recv, part_send, part_recv, ss_sems, pg_send, pg_recv,
):
    f32, bf16 = jnp.float32, jnp.bfloat16
    rows, half_width = hs.shape[1], hs.shape[2]
    sub = half_width // NSUB
    x = lax.axis_index("groups")
    me = lax.axis_index("pool")
    t = lax.axis_index("tensor")
    z, y = me // 2, lax.rem(me, 2)
    ox, oy, ot = 1 - x, 1 - y, 1 - t
    depth = 4

    def device(g, p, c):
        return {"groups": g, "pool": p, "tensor": c}

    x_peer = device(ox, me, t)
    y_peer = device(x, z * 2 + oy, t)
    up_peer = device(x, jnp.minimum(z + 1, depth - 1) * 2 + y, t)
    down_peer = device(x, jnp.maximum(z - 1, 0) * 2 + y, t)
    t_peer = device(x, me, ot)
    has_up, has_down = z < depth - 1, z > 0

    blocks = h_sem.shape[0]
    block_rows = rows // blocks

    def hidden_copy(b):
        window = pl.ds(b * block_rows, block_rows)
        return pltpu.make_async_copy(h_ref.at[window], hraw.at[window], h_sem.at[b])

    for b in range(blocks):
        hidden_copy(b).start()
    own_copy = pltpu.make_async_copy(w_ref, wbuf.at[me], own_sem)
    own_copy.start()

    barrier = pltpu.get_barrier_semaphore()
    for o in range(1, 8):
        pl.semaphore_signal(
            barrier, inc=1, device_id=device(x, lax.rem(me + o, 8), t), device_id_type=MESH
        )
    pl.semaphore_signal(barrier, inc=1, device_id=x_peer, device_id_type=MESH)
    pl.semaphore_signal(barrier, inc=1, device_id=t_peer, device_id_type=MESH)
    pl.semaphore_wait(barrier, 9)

    started = []

    def window(h, s):
        return pl.ds(pl.multiple_of(h * half_width + s * sub, sub), sub)

    def piece(slot, h, s):
        return wbuf.at[slot, window(h, s), :]

    def copy_of(way, slot, h, s, peer, own=False):
        source = w_ref.at[window(h, s), :] if own else piece(slot, h, s)
        return pltpu.make_async_remote_copy(
            src_ref=source,
            dst_ref=piece(slot, h, s),
            send_sem=w_send.at[way, slot, h, s],
            recv_sem=w_recv.at[slot, h, s],
            device_id=peer,
            device_id_type=MESH,
        )

    def send(way, slot, h, s, peer, cond=None, own=False):
        copy = copy_of(way, slot, h, s, peer, own)
        started.append((cond, copy))
        if cond is None:
            copy.start()
        else:
            pl.when(cond)(copy.start)

    def arrive(slot, h, s):
        copy_of(2, slot, h, s, x_peer).wait_recv()

    for s in range(NSUB):
        send(0, me, x, s, up_peer, has_up, own=True)
        send(1, me, x, s, down_peer, has_down, own=True)
        send(3, me, x, s, y_peer, own=True)

    gain = gain_ref[...].astype(f32)

    step_rows = 16

    def scale_block(b):
        hidden_copy(b).wait()

        @pl.loop(0, block_rows // step_rows)
        def _(i):
            at = pl.ds(pl.multiple_of(b * block_rows + i * step_rows, step_rows), step_rows)
            wide = hraw[at, :].astype(f32)
            scaled = (wide * gain).astype(bf16)
            hs[0, at, :] = scaled[:, :half_width]
            hs[1, at, :] = scaled[:, half_width:]
            total = jnp.sum(wide * wide, axis=1, keepdims=True)
            ss_send[at, :] = jnp.broadcast_to(total, (step_rows, HEAD_WIDTH))

    for b in range(blocks // 2):
        scale_block(b)

    low = z < depth // 2
    mirrored = jnp.where(low, z, depth - 1 - z)

    def plane(k):
        o = 1 - mirrored if k == 0 else k + 1
        return jnp.where(low, o, depth - 1 - o)

    def on_z(k):
        zk = plane(k)
        slot = zk * 2 + y
        for s in range(NSUB):
            arrive(slot, x, s)
            if k < 2:
                send(0, slot, x, s, up_peer, (zk < z) & has_up)
                send(1, slot, x, s, down_peer, (zk > z) & has_down)
            else:
                send(0, slot, x, s, up_peer, (zk < z) & has_up)
                send(1, slot, x, s, down_peer, (zk > z) & has_down)
            send(2, slot, x, s, x_peer)
            send(3, slot, x, s, y_peer)

    def on_y(k):
        slot = plane(k) * 2 + oy
        for s in range(NSUB):
            arrive(slot, x, s)
            send(2, slot, x, s, x_peer)

    def wait_all(slot, h):
        for s in range(NSUB):
            arrive(slot, h, s)

    def multiply(slot, h, first):
        @pl.loop(0, rows // 256)
        def _(r):
            at = pl.ds(pl.multiple_of(r * 256, 256), 256)
            part = jnp.dot(
                hs[h, at, :],
                wbuf[slot, pl.ds(pl.multiple_of(h * half_width, half_width), half_width), :],
                preferred_element_type=f32,
            )
            if first:
                accs[slot, at, :] = part
            else:
                accs[slot, at, :] = accs[slot, at, :] + part

    def part_copy(slot):
        at = lax.rem(slot, 4)
        return pltpu.make_async_remote_copy(
            src_ref=psend_buf.at[at],
            dst_ref=precv_buf.at[at],
            send_sem=part_send.at[at],
            recv_sem=part_recv.at[at],
            device_id=t_peer,
            device_id_type=MESH,
        )

    def complete(slot):
        @pl.when(slot // 4 != t)
        def _():
            psend_buf[lax.rem(slot, 4)] = accs[slot].astype(bf16)
            part_copy(slot).start()

    page_len = page_ref.shape[1]

    @pl.loop(0, 8)
    def _(d):
        taken = [(req_ref[i] == d).astype(f32) for i in range(page_ref.shape[0])]
        for c in range(0, page_len, 32):
            total = page_ref[0, c : c + 32, :].astype(f32) * taken[0]
            for i in range(1, page_ref.shape[0]):
                total = total + page_ref[i, c : c + 32, :].astype(f32) * taken[i]
            pout[d, c : c + 32, :] = total.astype(bf16)
        flag = taken[0] + taken[1] + taken[2] + taken[3]
        pout[d, page_len:, :] = jnp.full((FLAG_ROWS, pout.shape[2]), 1.0, f32).astype(bf16) * flag.astype(bf16)

    on_z(0)

    for b in range(blocks // 2, blocks):
        scale_block(b)
    ss_copy = pltpu.make_async_remote_copy(
        src_ref=ss_send,
        dst_ref=ss_recv,
        send_sem=ss_sems.at[0],
        recv_sem=ss_sems.at[1],
        device_id=t_peer,
        device_id_type=MESH,
    )
    ss_copy.start()

    self_page = pltpu.make_async_copy(pout.at[me], pin.at[me], page_self_sem)
    self_page.start()

    def page_copy(o, source, target):
        return pltpu.make_async_remote_copy(
            src_ref=pout.at[target],
            dst_ref=pin.at[source],
            send_sem=pg_send.at[o],
            recv_sem=pg_recv.at[o],
            device_id=device(x, target, t),
            device_id_type=MESH,
        )

    page_sends = []
    for o in range(1, 8):
        copy = page_copy(o, me, lax.rem(me + o, 8))
        copy.start()
        page_sends.append(copy)

    on_z(1)
    own_copy.wait()
    multiply(me, 0, True)
    on_y(0)
    on_z(2)
    multiply(me, 1, False)
    complete(me)
    for s in range(NSUB):
        send(3, me, ox, s, y_peer, own=True)
    wait_all(z * 2 + oy, x)
    multiply(z * 2 + oy, x, True)
    multiply(plane(0) * 2 + y, x, True)
    on_y(1)
    wait_all(plane(0) * 2 + y, ox)
    multiply(plane(0) * 2 + y, ox, False)
    complete(plane(0) * 2 + y)
    multiply(plane(0) * 2 + oy, x, True)
    on_y(2)
    multiply(plane(1) * 2 + y, x, True)
    multiply(plane(1) * 2 + oy, x, True)
    multiply(plane(2) * 2 + y, x, True)
    multiply(plane(2) * 2 + oy, x, True)

    heads = 2
    fresh = q_ref.shape[0]
    group_rows = HEADS_PER_GROUP * fresh
    scale = HEAD_WIDTH ** (-0.5)
    for j in range(heads):
        for g in range(HEADS_PER_GROUP):
            at = (j * HEADS_PER_GROUP + g) * HEAD_WIDTH
            qbuf[j, g * fresh : (g + 1) * fresh, :] = q_ref[:, at : at + HEAD_WIDTH]

    def inner(a, b):
        return lax.dot_general(a, b, (((1,), (1,)), ((), ())), preferred_element_type=f32)

    self_page.wait()
    for o in range(1, 8):
        page_copy(o, lax.rem(me + 8 - o, 8), me).wait_recv()
    flags = jnp.concatenate(
        [pin[i, page_len:, :HEAD_WIDTH].astype(f32)[:1, :] for i in range(8)], axis=1
    )
    for j in range(heads):
        kc, vc = j * HEAD_WIDTH, (heads + j) * HEAD_WIDTH
        query = qbuf[j]
        near = inner(query, nkv_ref[:, kc : kc + HEAD_WIDTH]) * scale
        row_at = lax.rem(lax.broadcasted_iota(jnp.int32, near.shape, 0), fresh)
        near = jnp.where(lax.broadcasted_iota(jnp.int32, near.shape, 1) <= row_at, near, MASKED)
        keys = pin[:, :page_len, kc : kc + HEAD_WIDTH].reshape(8 * page_len, HEAD_WIDTH)
        values = pin[:, :page_len, vc : vc + HEAD_WIDTH].reshape(8 * page_len, HEAD_WIDTH)
        far = jnp.where(flags > 0.5, inner(query, keys) * scale, MASKED)
        high = jnp.maximum(
            jnp.max(near, axis=1, keepdims=True), jnp.max(far, axis=1, keepdims=True)
        )
        near, far = jnp.exp(near - high), jnp.exp(far - high)
        mass = jnp.sum(near, axis=1, keepdims=True) + jnp.sum(far, axis=1, keepdims=True)
        m_st[j] = jnp.broadcast_to(high, (group_rows, HEAD_WIDTH))
        l_st[j] = jnp.broadcast_to(mass, (group_rows, HEAD_WIDTH))
        a_st[j] = jnp.dot(
            near.astype(bf16), nkv_ref[:, vc : vc + HEAD_WIDTH], preferred_element_type=f32
        ) + jnp.dot(far.astype(bf16), values, preferred_element_type=f32)

    ss_copy.wait()

    @pl.loop(0, rows // 128)
    def _(r):
        at = pl.ds(pl.multiple_of(r * 128, 128), 128)
        ss_send[at, :] = lax.rsqrt((ss_send[at, :] + ss_recv[at, :]) / MODEL_WIDTH + epsilon)

    half = HEAD_WIDTH // 2

    def finish(j):
        slot = (2 * t + j) * 2
        for c in range(2):
            part_copy(slot + c).wait_recv()
        bias = jnp.where(j == 0, bias_ref[:, :HEAD_WIDTH].astype(f32), bias_ref[:, HEAD_WIDTH:].astype(f32))

        @pl.loop(0, rows // 128)
        def _(r):
            at = pl.ds(pl.multiple_of(r * 128, 128), 128)
            lead = accs[slot, at, :] + precv_buf[2 * j, at, :].astype(f32)
            tail = accs[slot + 1, at, :] + precv_buf[2 * j + 1, at, :].astype(f32)
            inverse = ss_send[at, :]
            key = jnp.concatenate([lead[:, :half], tail[:, :half]], axis=1) * inverse + bias[0:1]
            value = jnp.concatenate([lead[:, half:], tail[:, half:]], axis=1) * inverse + bias[1:2]
            turned = jnp.concatenate([key[:, half:], key[:, :half]], axis=1)
            kbuf[at, :] = (key * cos_ref[at, :] + turned * sin_ref[at, :]).astype(bf16)
            vbuf[at, :] = value.astype(bf16)

        scores = inner(qbuf[j], kbuf[...]) * scale
        seen = lax.broadcasted_iota(jnp.int32, scores.shape, 1) < plen_ref[0]
        scores = jnp.where(seen, scores, MASKED)
        before = m_st[j][:, :1]
        high = jnp.maximum(before, jnp.max(scores, axis=1, keepdims=True))
        weights = jnp.exp(scores - high)
        factor = jnp.exp(before - high)
        mass = l_st[j][:, :1] * factor + jnp.sum(weights, axis=1, keepdims=True)
        total = a_st[j] * factor + jnp.dot(
            weights.astype(bf16), vbuf[...], preferred_element_type=f32
        )
        obuf[j] = (total / mass).astype(bf16)

    def last_of(k, column):
        slot = plane(k) * 2 + column
        wait_all(slot, ox)
        multiply(slot, ox, False)
        complete(slot)

    last_of(0, oy)
    last_of(1, y)
    wait_all(z * 2 + oy, ox)
    multiply(z * 2 + oy, ox, False)
    complete(z * 2 + oy)
    last_of(1, oy)
    finish(jnp.where(low, 0, 1))
    last_of(2, y)
    last_of(2, oy)
    finish(jnp.where(low, 1, 0))

    for j in range(heads):
        for g in range(HEADS_PER_GROUP):
            at = (j * HEADS_PER_GROUP + g) * HEAD_WIDTH
            out_ref[:, at : at + HEAD_WIDTH] = obuf[j, g * fresh : (g + 1) * fresh, :]

    for cond, copy in started:
        if cond is None:
            copy.wait_send()
        else:
            pl.when(cond)(copy.wait_send)
    for copy in page_sends:
        copy.wait_send()
    for i in range(4):
        part_copy(4 * ot + i).wait_send()


def fused(
    hidden, norm_gain, key_value_weight, key_value_bias, stored_page_pool, page_request, prefix_len,
    queries, new_key_value,
):
    rows, width = hidden.shape
    fresh = queries.shape[0]
    pages, page_len = stored_page_pool.shape[:2]
    cosine, sine = rotation_tables(rows)
    vmem = pl.BlockSpec(memory_space=pltpu.VMEM)
    smem = pl.BlockSpec(memory_space=pltpu.SMEM)
    anywhere = pl.BlockSpec(memory_space=pl.ANY)
    bf16, f32 = jnp.bfloat16, jnp.float32
    dma = pltpu.SemaphoreType.DMA
    return pl.pallas_call(
        fused_kernel,
        out_shape=jax.ShapeDtypeStruct(queries.shape, bf16),
        in_specs=[anywhere, anywhere, vmem, vmem, vmem, smem, smem, vmem, vmem, vmem, vmem],
        out_specs=vmem,
        scratch_shapes=[
            pltpu.VMEM((8, width, HEAD_WIDTH), bf16),
            pltpu.VMEM((rows, width), bf16),
            pltpu.VMEM((2, rows, width // 2), bf16),
            pltpu.VMEM((8, rows, HEAD_WIDTH), f32),
            pltpu.VMEM((4, rows, HEAD_WIDTH), bf16),
            pltpu.VMEM((4, rows, HEAD_WIDTH), bf16),
            pltpu.VMEM((rows, HEAD_WIDTH), f32),
            pltpu.VMEM((rows, HEAD_WIDTH), f32),
            pltpu.VMEM((8, page_len + FLAG_ROWS, 4 * HEAD_WIDTH), bf16),
            pltpu.VMEM((8, page_len + FLAG_ROWS, 4 * HEAD_WIDTH), bf16),
            pltpu.VMEM((2, HEADS_PER_GROUP * fresh, HEAD_WIDTH), bf16),
            pltpu.VMEM((rows, HEAD_WIDTH), bf16),
            pltpu.VMEM((rows, HEAD_WIDTH), bf16),
            pltpu.VMEM((2, HEADS_PER_GROUP * fresh, HEAD_WIDTH), bf16),
            pltpu.VMEM((2, HEADS_PER_GROUP * fresh, HEAD_WIDTH), f32),
            pltpu.VMEM((2, HEADS_PER_GROUP * fresh, HEAD_WIDTH), f32),
            pltpu.VMEM((2, HEADS_PER_GROUP * fresh, HEAD_WIDTH), f32),
            dma((8,)), dma, dma,
            dma((4, 8, 2, NSUB)), dma((8, 2, NSUB)),
            dma((4,)), dma((4,)), dma((2,)), dma((8,)), dma((8,)),
        ],
        compiler_params=pltpu.CompilerParams(
            collective_id=0, has_side_effects=True, vmem_limit_bytes=56 * 1024 * 1024
        ),
    )(
        key_value_weight.reshape(width, HEAD_WIDTH),
        hidden,
        norm_gain.reshape(1, width),
        key_value_bias,
        stored_page_pool.reshape(pages, page_len, 4 * HEAD_WIDTH),
        page_request,
        prefix_len,
        queries,
        new_key_value.reshape(fresh, 4 * HEAD_WIDTH),
        jnp.asarray(cosine),
        jnp.asarray(sine),
    )


def solution(mesh):
    shape = dict(mesh.shape)
    small = shape["pool"] == 8 and shape["groups"] == 2 and shape["tensor"] == 2
    return jax.shard_map(
        fused if small else local,
        mesh=mesh,
        in_specs=(
            P(("groups", "pool"), "tensor"),
            P("tensor"),
            P("tensor", None, "pool"),
            P(None, "tensor"),
            P(("groups", "pool"), None, None, "tensor"),
            P(("groups", "pool")),
            P(("groups", "pool")),
            P(("groups", "pool"), "tensor"),
            P(("groups", "pool"), None, "tensor"),
        ),
        out_specs=P(("groups", "pool"), "tensor"),
        check_vma=False,
    )
```

```python
import functools
import math

import numpy as np
import jax
import jax.numpy as jnp
from jax import lax
from jax.experimental import pallas as pl
from jax.experimental.pallas import tpu as pltpu
from jax.sharding import PartitionSpec as P

MODEL_WIDTH = 8192
HEADS_PER_GROUP = 8
HEAD_WIDTH = 128
CAP = 1


rope_base = 1000000.0
epsilon = 1e-06
MESH = pl.DeviceIdType.MESH


def apply_rotation(key_portion, token_positions):
    half_dim = key_portion.shape[-1] // 2
    frequency = rope_base ** (
        -(jnp.arange(half_dim, dtype=jnp.float32) * 2.0 / key_portion.shape[-1])
    )
    angles = token_positions.astype(jnp.float32)[:, None] * frequency[None, :]
    cosine = jnp.cos(angles)[:, None, :]
    sine_part = jnp.sin(angles)[:, None, :]
    lead_half = key_portion[..., :half_dim]
    tail_half = key_portion[..., half_dim:]
    return jnp.concatenate(
        [lead_half * cosine - tail_half * sine_part, tail_half * cosine + lead_half * sine_part],
        axis=-1,
    )


def absorb(running, query_heads, key_portion, value_part, visible):
    highest, mass_sum, weighted = running
    scores = jnp.einsum(
        "hgqd,khd->hgqk", query_heads, key_portion, preferred_element_type=jnp.float32
    ) * query_heads.shape[-1] ** (-0.5)
    scores = jnp.where(visible, scores, -jnp.inf)
    new_high = jnp.maximum(highest, jnp.max(scores, axis=-1))
    anchor = jnp.where(jnp.isfinite(new_high), new_high, 0.0)
    prob_rows = jnp.exp(scores - anchor[..., None])
    factor = jnp.exp(highest - anchor)
    mass_sum = mass_sum * factor + jnp.sum(prob_rows, axis=-1)
    weighted = weighted * factor[..., None] + jnp.einsum(
        "hgqk,khd->hgqd",
        prob_rows.astype(jnp.bfloat16),
        value_part,
        preferred_element_type=jnp.float32,
    )
    return (new_high, mass_sum, weighted)


def local(
    hidden,
    norm_gain,
    key_value_weight,
    key_value_bias,
    stored_page_pool,
    page_request,
    prefix_len,
    queries,
    new_key_value,
):
    row_count = hidden.shape[0]
    wide_hidden = hidden.astype(jnp.float32)
    scaled_scores = (wide_hidden * norm_gain.astype(jnp.float32)[None, :]).astype(jnp.bfloat16)
    local_squares = jnp.sum(wide_hidden * wide_hidden, axis=1)
    piece = lax.all_gather(key_value_weight, "pool", axis=2, tiled=True)
    width_part = piece.shape[2]
    product = jnp.dot(
        scaled_scores,
        piece.reshape(piece.shape[0], 2 * width_part),
        preferred_element_type=jnp.float32,
    )
    partial_value = product.reshape(row_count, 2, width_part)
    squares = lax.psum(local_squares, "tensor")
    projected_hidden = lax.psum_scatter(
        partial_value.astype(jnp.bfloat16), "tensor", scatter_dimension=2, tiled=True
    ).astype(jnp.float32)
    inverse_frequency = lax.rsqrt(squares / MODEL_WIDTH + epsilon)
    local_heads = projected_hidden.shape[2] // HEAD_WIDTH
    kv_rows = (
        inverse_frequency[:, None, None] * projected_hidden
        + key_value_bias.astype(jnp.float32)[None]
    )
    kv_rows = kv_rows.reshape(row_count, 2, local_heads, HEAD_WIDTH)
    token_positions = jnp.arange(row_count, dtype=jnp.int32)
    restored_prefix_keys = apply_rotation(kv_rows[:, 0], token_positions).astype(jnp.bfloat16)
    restored_prefix_values = kv_rows[:, 1].astype(jnp.bfloat16)
    fresh_count = queries.shape[0]
    query_heads = queries.reshape(fresh_count, local_heads, HEADS_PER_GROUP, HEAD_WIDTH).transpose(
        1, 2, 0, 3
    )
    fresh_keys = new_key_value[:, 0].reshape(fresh_count, local_heads, HEAD_WIDTH)
    fresh_values = new_key_value[:, 1].reshape(fresh_count, local_heads, HEAD_WIDTH)
    prefix_ok = token_positions < prefix_len[0]
    causal = jnp.arange(fresh_count)[None, :] <= jnp.arange(fresh_count)[:, None]
    visible = jnp.concatenate(
        [jnp.broadcast_to(prefix_ok[None, :], (fresh_count, row_count)), causal], axis=1
    )
    start_state = (
        jnp.full((local_heads, HEADS_PER_GROUP, fresh_count), -jnp.inf, jnp.float32),
        jnp.zeros((local_heads, HEADS_PER_GROUP, fresh_count), jnp.float32),
        jnp.zeros((local_heads, HEADS_PER_GROUP, fresh_count, HEAD_WIDTH), jnp.float32),
    )
    running = absorb(
        start_state,
        query_heads,
        jnp.concatenate([restored_prefix_keys, fresh_keys], axis=0),
        jnp.concatenate([restored_prefix_values, fresh_values], axis=0),
        visible,
    )
    page_count = page_request.shape[0]
    page_index = jnp.arange(page_count)
    same_request = (page_request[:, None] == page_request[None, :]) & (
        page_index[None, :] < page_index[:, None]
    )
    slot_rank = jnp.sum(same_request.astype(jnp.int32), axis=1)
    pool_size = lax.axis_size("pool")
    page_len = stored_page_pool.shape[1]
    outgoing = (
        jnp.zeros((pool_size, CAP) + stored_page_pool.shape[1:], jnp.bfloat16)
        .at[page_request, slot_rank]
        .set(stored_page_pool)
    )
    occupied = jnp.zeros((pool_size, CAP), jnp.bfloat16).at[page_request, slot_rank].set(1.0)
    arrived, present = (
        lax.all_to_all(outgoing, "pool", split_axis=0, concat_axis=0, tiled=True),
        lax.all_to_all(occupied, "pool", split_axis=0, concat_axis=0, tiled=True),
    )
    slot_total_count = pool_size * CAP
    per_block = math.gcd(slot_total_count, max(1, 1024 // page_len))
    grouped = arrived.reshape(
        slot_total_count // per_block, per_block * page_len, 2, local_heads, HEAD_WIDTH
    )
    live_keys = (
        jnp.repeat(present.reshape(slot_total_count // per_block, per_block), page_len, axis=1)
        > 0.5
    )

    def visit_block(carried, scan_item):
        page_block, is_live = scan_item
        return (
            absorb(carried, query_heads, page_block[:, 0], page_block[:, 1], is_live[None, :]),
            None,
        )

    running, unused = lax.scan(visit_block, running, (grouped, live_keys))
    highest, mass_sum, weighted = running
    attended = weighted / mass_sum[..., None]
    return attended.transpose(2, 0, 1, 3).reshape(fresh_count, -1).astype(jnp.bfloat16)


PIECES = 8
ALONG_Z = 5
ALONG_Y = 4
PLANE_Y = 6
REST_AT = 9
PAGES_AT = 12
FIRST_AT = 10
AT_ONCE = (2, 2, 99, 99)
MASKED = -1e30
FLAG_ROWS = 16


def rotation_tables(row_count):
    half = HEAD_WIDTH // 2
    frequency = rope_base ** (-(np.arange(half, dtype=np.float64) * 2.0 / HEAD_WIDTH))
    angles = np.arange(row_count, dtype=np.float64)[:, None] * frequency[None, :]
    cosine, sine = np.cos(angles), np.sin(angles)
    return (
        np.concatenate([cosine, cosine], axis=1).astype(np.float32),
        np.concatenate([-sine, sine], axis=1).astype(np.float32),
    )


def fused_kernel(
    w_ref, h_ref, gain_ref, bias_ref, page_ref, req_ref, plen_ref, q_ref, nkv_ref, cos_ref, sin_ref,
    out_ref,
    wbuf, hraw, hs, accs, psend_buf, precv_buf, ss_send, ss_recv, pout, pin, qbuf, kbuf, vbuf, obuf,
    m_st, l_st, a_st, flat_pages,
    h_sem, own_sem, page_self_sem, w_send, w_recv, part_send, part_recv, ss_sems, pg_send, pg_recv,
):
    f32, bf16 = jnp.float32, jnp.bfloat16
    rows, sub = hs.shape[1], hs.shape[2]
    x = lax.axis_index("groups")
    me = lax.axis_index("pool")
    t = lax.axis_index("tensor")
    z, y = me // 2, lax.rem(me, 2)
    ox, oy, ot = 1 - x, 1 - y, 1 - t
    depth = 4

    def device(g, p, c):
        return {"groups": g, "pool": p, "tensor": c}

    x_peer = device(ox, me, t)
    y_peer = device(x, z * 2 + oy, t)
    low = z < depth // 2
    inside = (z > 0) & (z < depth - 1)
    up, down = jnp.minimum(z + 1, depth - 1), jnp.maximum(z - 1, 0)
    far_peer = device(x, jnp.where(low, up, down) * 2 + y, t)
    near_peer = device(x, jnp.where(low, down, up) * 2 + y, t)
    t_peer = device(x, me, ot)

    blocks = h_sem.shape[0]
    block_rows = rows // blocks

    def hidden_copy(b):
        window = pl.ds(b * block_rows, block_rows)
        return pltpu.make_async_copy(h_ref.at[window], hraw.at[window], h_sem.at[b])

    for b in range(blocks):
        hidden_copy(b).start()
    own_copies = [
        pltpu.make_async_copy(w_ref.at[:, pl.ds(i * sub, sub)], wbuf.at[me, i], own_sem.at[i])
        for i in range(PIECES)
    ]
    for copy in own_copies:
        copy.start()

    barrier = pltpu.get_barrier_semaphore()
    for o in range(1, 8):
        pl.semaphore_signal(
            barrier, inc=1, device_id=device(x, lax.rem(me + o, 8), t), device_id_type=MESH
        )
    pl.semaphore_signal(barrier, inc=1, device_id=x_peer, device_id_type=MESH)
    pl.semaphore_signal(barrier, inc=1, device_id=t_peer, device_id_type=MESH)
    pl.semaphore_wait(barrier, 9)

    def nth(r):
        return jnp.where(x == 0, r, PIECES - 1 - r)

    def copy_of(way, slot, r, peer):
        piece = nth(r)
        return pltpu.make_async_remote_copy(
            src_ref=wbuf.at[slot, piece],
            dst_ref=wbuf.at[slot, piece],
            send_sem=w_send.at[way, slot, piece],
            recv_sem=w_recv.at[slot, piece],
            device_id=peer,
            device_id_type=MESH,
        )

    in_flight = [[] for _ in AT_ONCE]

    def run_if(cond, do):
        if cond is None:
            do()
        else:
            pl.when(cond)(do)

    def send(way, slot, r, peer, cond=None):
        queue = in_flight[way]
        if len(queue) >= AT_ONCE[way]:
            before, earlier = queue.pop(0)
            run_if(before, earlier.wait_send)
        copy = copy_of(way, slot, r, peer)
        queue.append((cond, copy))
        run_if(cond, copy.start)

    def arrive(slot, r):
        copy_of(2, slot, r, x_peer).wait_recv()

    for copy in own_copies:
        copy.wait()
    def send_own(r):
        send(1, me, r, near_peer, inside)
        send(0, me, r, far_peer)

    for r in range(2):
        send_own(r)
        if r < PIECES - PLANE_Y:
            send(3, me, r, y_peer)

    gain = gain_ref[...].astype(f32).reshape(1, PIECES * sub)

    step_rows = 16

    def scale_block(b):
        hidden_copy(b).wait()

        @pl.loop(0, block_rows // step_rows)
        def _(i):
            at = pl.ds(pl.multiple_of(b * block_rows + i * step_rows, step_rows), step_rows)
            wide = hraw[at, :].astype(f32)
            scaled = (wide * gain).astype(bf16)
            for i in range(PIECES):
                hs[i, at, :] = scaled[:, i * sub : (i + 1) * sub]
            total = jnp.sum(wide * wide, axis=1, keepdims=True)
            ss_send[at, :] = jnp.broadcast_to(total, (step_rows, HEAD_WIDTH))

    mirrored = jnp.where(low, z, depth - 1 - z)

    def plane(k):
        o = 1 - mirrored if k == 0 else k + 1
        return jnp.where(low, o, depth - 1 - o)

    here_y, there_y = lambda k: plane(k) * 2 + y, lambda k: plane(k) * 2 + oy
    plane_y = z * 2 + oy

    def on_z(k, r):
        slot = here_y(k)
        arrive(slot, r)
        if k > 0:
            send(1, slot, r, near_peer, inside)
        if r < ALONG_Y:
            send(3, slot, r, y_peer)
        if r < PIECES - ALONG_Z:
            send(2, slot, r, x_peer)
        if k == 0 and r + 2 < ALONG_Z:
            send_own(r + 2)
        if k == 1:
            send(0, here_y(0), r, far_peer, inside)

    def on_y(k, r):
        slot = there_y(k)
        arrive(slot, r)
        send(2, slot, r, x_peer)

    def on_plane(r):
        arrive(plane_y, r)
        send(2, plane_y, r, x_peer)

    def multiply(p, pieces, first):
        @pl.loop(0, rows // 256)
        def _(b):
            at = pl.ds(pl.multiple_of(b * 256, 256), 256)
            total = None if first else accs[p, at, :]
            for r in pieces:
                shards = wbuf[pl.ds(p * 2, 2), nth(r)].reshape(2 * HEAD_WIDTH, sub)
                part = lax.dot_general(
                    hs[nth(r), at, :], shards, (((1,), (1,)), ((), ())), preferred_element_type=f32
                )
                total = part if total is None else total + part
            accs[p, at, :] = total

    def part_copy(p):
        at = lax.rem(p, 2)
        return pltpu.make_async_remote_copy(
            src_ref=psend_buf.at[at],
            dst_ref=precv_buf.at[at],
            send_sem=part_send.at[at],
            recv_sem=part_recv.at[at],
            device_id=t_peer,
            device_id_type=MESH,
        )

    def complete(p):
        @pl.when(p // 2 != t)
        def _():
            psend_buf[lax.rem(p, 2)] = accs[p].astype(bf16)
            part_copy(p).start()

    page_len = page_ref.shape[1]
    heads = 2
    width = heads * HEAD_WIDTH

    def pack(d):
        taken = [(req_ref[i] == d).astype(f32) for i in range(page_ref.shape[0])]
        for c in range(0, page_len, 32):
            total = flat_pages[0, c : c + 32, :].astype(f32) * taken[0]
            for i in range(1, page_ref.shape[0]):
                total = total + flat_pages[i, c : c + 32, :].astype(f32) * taken[i]
            pout[d, c : c + 32, :] = total.astype(bf16)
        flag = sum(taken[1:], taken[0])
        pout[d, page_len:, :] = (jnp.full((FLAG_ROWS, pout.shape[2]), 1.0, f32) * flag).astype(bf16)

    def page_copy(o, source, target):
        return pltpu.make_async_remote_copy(
            src_ref=pout.at[target],
            dst_ref=pin.at[source],
            send_sem=pg_send.at[o],
            recv_sem=pg_recv.at[o],
            device_id=device(x, target, t),
            device_id_type=MESH,
        )

    self_page = pltpu.make_async_copy(pout.at[me], pin.at[me], page_self_sem)
    page_sends = [page_copy(o, me, lax.rem(me + o, 8)) for o in range(1, 8)]
    ss_copy = pltpu.make_async_remote_copy(
        src_ref=ss_send,
        dst_ref=ss_recv,
        send_sem=ss_sems.at[0],
        recv_sem=ss_sems.at[1],
        device_id=t_peer,
        device_id_type=MESH,
    )

    def flatten(i):
            for c in range(0, page_len, 32):
                wide = page_ref[i, c : c + 32].astype(f32)
                flat_pages[i, c : c + 32, :width] = wide[:, 0, :].astype(bf16)
                flat_pages[i, c : c + 32, width:] = wide[:, 1, :].astype(bf16)

    def send_pages():
        self_page.start()
        for copy in page_sends:
            copy.start()

    def rest_of_plane():
        for r in range(PIECES - PLANE_Y, PLANE_Y):
            send(3, me, r, y_peer)

    beside = {}

    def then(n, *work):
        beside.setdefault(n, []).extend(work)

    for b in range(blocks):
        then(b, functools.partial(scale_block, b))
    for i in range(page_ref.shape[0]):
        then(i, functools.partial(flatten, i))
    for d in range(8):
        then(4 + d // 2, functools.partial(pack, d))
    then(blocks, ss_copy.start)
    then(REST_AT, rest_of_plane)
    then(PAGES_AT, send_pages)
    for i in range(4):
        then(FIRST_AT + i, functools.partial(multiply, plane(0), (i,), i == 0))

    for r in range(PIECES - PLANE_Y):
        on_plane(r)
    lag = 2
    for n in range(3 * ALONG_Z + 3):
        if n < 3 * ALONG_Z:
            on_z(n // ALONG_Z, n % ALONG_Z)
        k, r = (n - lag) // ALONG_Z, (n - lag) % ALONG_Z
        if n >= lag and k < 3 and r < ALONG_Y:
            on_y(k, r)
        for work in beside.get(n, []):
            work()

    fresh = q_ref.shape[0]
    group_rows = HEADS_PER_GROUP * fresh
    scale = HEAD_WIDTH ** (-0.5)
    for j in range(heads):
        for g in range(HEADS_PER_GROUP):
            at = (j * HEADS_PER_GROUP + g) * HEAD_WIDTH
            qbuf[j, g * fresh : (g + 1) * fresh, :] = q_ref[:, at : at + HEAD_WIDTH]

    def inner(a, b):
        return lax.dot_general(a, b, (((1,), (1,)), ((), ())), preferred_element_type=f32)

    def absorb(j, scores, values, first=False):
        high = jnp.max(scores, axis=1, keepdims=True)
        if not first:
            before = m_st[j][:, :1]
            high = jnp.maximum(before, high)
        weights = jnp.exp(scores - high)
        mass = jnp.broadcast_to(jnp.sum(weights, axis=1, keepdims=True), (group_rows, HEAD_WIDTH))
        total = jnp.dot(weights.astype(bf16), values, preferred_element_type=f32)
        if not first:
            factor = jnp.exp(before - high)
            mass = mass + l_st[j] * factor
            total = total + a_st[j] * factor
        m_st[j] = jnp.broadcast_to(high, (group_rows, HEAD_WIDTH))
        l_st[j] = mass
        a_st[j] = total

    fresh_wide = nkv_ref[...].astype(f32)
    new_keys, new_values = fresh_wide[:, 0, :].astype(bf16), fresh_wide[:, 1, :].astype(bf16)
    for j in range(heads):
        kc = j * HEAD_WIDTH
        near = inner(qbuf[j], new_keys[:, kc : kc + HEAD_WIDTH]) * scale
        row_at = lax.rem(lax.broadcasted_iota(jnp.int32, near.shape, 0), fresh)
        near = jnp.where(lax.broadcasted_iota(jnp.int32, near.shape, 1) <= row_at, near, MASKED)
        absorb(j, near, new_values[:, kc : kc + HEAD_WIDTH], True)

    def pages_in():
        self_page.wait()
        for o in range(1, 8):
            page_copy(o, lax.rem(me + 8 - o, 8), me).wait_recv()
        flags = jnp.concatenate(
            [pin[i, page_len:, :HEAD_WIDTH].astype(f32)[:1, :] for i in range(8)], axis=1
        )
        for j in range(heads):
            kc, vc = j * HEAD_WIDTH, (heads + j) * HEAD_WIDTH
            keys = pin[:, :page_len, kc : kc + HEAD_WIDTH].reshape(8 * page_len, HEAD_WIDTH)
            values = pin[:, :page_len, vc : vc + HEAD_WIDTH].reshape(8 * page_len, HEAD_WIDTH)
            absorb(j, jnp.where(flags > 0.5, inner(qbuf[j], keys) * scale, MASKED), values)

    def norms():
        ss_copy.wait()

        @pl.loop(0, rows // 128)
        def _(r):
            at = pl.ds(pl.multiple_of(r * 128, 128), 128)
            ss_send[at, :] = lax.rsqrt((ss_send[at, :] + ss_recv[at, :]) / MODEL_WIDTH + epsilon)

    half = HEAD_WIDTH // 2

    def finish(j):
        p = 2 * t + j
        part_copy(p).wait_recv()
        bias = jnp.where(j == 0, bias_ref[:, :HEAD_WIDTH].astype(f32), bias_ref[:, HEAD_WIDTH:].astype(f32))

        @pl.loop(0, rows // 128)
        def _(r):
            at = pl.ds(pl.multiple_of(r * 128, 128), 128)
            both = accs[p, at, :] + precv_buf[j, at, :].astype(f32)
            lead, tail = both[:, :HEAD_WIDTH], both[:, HEAD_WIDTH:]
            inverse = ss_send[at, :]
            key = jnp.concatenate([lead[:, :half], tail[:, :half]], axis=1) * inverse + bias[0:1]
            value = jnp.concatenate([lead[:, half:], tail[:, half:]], axis=1) * inverse + bias[1:2]
            turned = jnp.concatenate([key[:, half:], key[:, :half]], axis=1)
            kbuf[at, :] = (key * cos_ref[at, :] + turned * sin_ref[at, :]).astype(bf16)
            vbuf[at, :] = value.astype(bf16)

        scores = inner(qbuf[j], kbuf[...]) * scale
        seen = lax.broadcasted_iota(jnp.int32, scores.shape, 1) < plen_ref[0]
        absorb(j, jnp.where(seen, scores, MASKED), vbuf[...])

    def await_x(slot, first):
        for r in range(PIECES - 1, first - 1, -1):
            arrive(slot, r)

    def close(k):
        await_x(here_y(k), ALONG_Z)
        await_x(there_y(k), ALONG_Y)
        multiply(plane(k), range(ALONG_Y, PIECES), False)
        complete(plane(k))

    norms()
    multiply(plane(1), range(ALONG_Y), True)
    for r in range(PIECES - PLANE_Y, PLANE_Y):
        arrive(plane_y, r)
    multiply(z, range(PLANE_Y), True)
    multiply(plane(2), range(ALONG_Y), True)
    await_x(plane_y, PLANE_Y)
    multiply(z, range(PLANE_Y, PIECES), False)
    complete(z)
    close(0)
    close(1)
    finish(jnp.where(low, 0, 1))
    pages_in()
    close(2)
    finish(jnp.where(low, 1, 0))

    for j in range(heads):
        obuf[j] = (a_st[j] / l_st[j]).astype(bf16)
    for j in range(heads):
        for g in range(HEADS_PER_GROUP):
            at = (j * HEADS_PER_GROUP + g) * HEAD_WIDTH
            out_ref[:, at : at + HEAD_WIDTH] = obuf[j, g * fresh : (g + 1) * fresh, :]

    for queue in in_flight:
        for cond, copy in queue:
            run_if(cond, copy.wait_send)
    for copy in page_sends:
        copy.wait_send()
    for i in range(2):
        part_copy(2 * ot + i).wait_send()


def fused(
    hidden, norm_gain, key_value_weight, key_value_bias, stored_page_pool, page_request, prefix_len,
    queries, new_key_value,
):
    rows, width = hidden.shape
    fresh = queries.shape[0]
    pages, page_len = stored_page_pool.shape[:2]
    cosine, sine = rotation_tables(rows)
    vmem = pl.BlockSpec(memory_space=pltpu.VMEM)
    smem = pl.BlockSpec(memory_space=pltpu.SMEM)
    anywhere = pl.BlockSpec(memory_space=pl.ANY)
    bf16, f32 = jnp.bfloat16, jnp.float32
    dma = pltpu.SemaphoreType.DMA
    return pl.pallas_call(
        fused_kernel,
        out_shape=jax.ShapeDtypeStruct(queries.shape, bf16),
        in_specs=[anywhere, anywhere, vmem, vmem, vmem, smem, smem, vmem, vmem, vmem, vmem],
        out_specs=vmem,
        scratch_shapes=[
            pltpu.VMEM((8, PIECES, HEAD_WIDTH, width // PIECES), bf16),
            pltpu.VMEM((rows, width), bf16),
            pltpu.VMEM((PIECES, rows, width // PIECES), bf16),
            pltpu.VMEM((4, rows, 2 * HEAD_WIDTH), f32),
            pltpu.VMEM((2, rows, 2 * HEAD_WIDTH), bf16),
            pltpu.VMEM((2, rows, 2 * HEAD_WIDTH), bf16),
            pltpu.VMEM((rows, HEAD_WIDTH), f32),
            pltpu.VMEM((rows, HEAD_WIDTH), f32),
            pltpu.VMEM((8, page_len + FLAG_ROWS, 4 * HEAD_WIDTH), bf16),
            pltpu.VMEM((8, page_len + FLAG_ROWS, 4 * HEAD_WIDTH), bf16),
            pltpu.VMEM((2, HEADS_PER_GROUP * fresh, HEAD_WIDTH), bf16),
            pltpu.VMEM((rows, HEAD_WIDTH), bf16),
            pltpu.VMEM((rows, HEAD_WIDTH), bf16),
            pltpu.VMEM((2, HEADS_PER_GROUP * fresh, HEAD_WIDTH), bf16),
            pltpu.VMEM((2, HEADS_PER_GROUP * fresh, HEAD_WIDTH), f32),
            pltpu.VMEM((2, HEADS_PER_GROUP * fresh, HEAD_WIDTH), f32),
            pltpu.VMEM((2, HEADS_PER_GROUP * fresh, HEAD_WIDTH), f32),
            pltpu.VMEM((pages, page_len, 4 * HEAD_WIDTH), bf16),
            dma((8,)), dma((PIECES,)), dma,
            dma((4, 8, PIECES)), dma((8, PIECES)),
            dma((2,)), dma((2,)), dma((2,)), dma((8,)), dma((8,)),
        ],
        compiler_params=pltpu.CompilerParams(
            collective_id=0, has_side_effects=True, vmem_limit_bytes=56 * 1024 * 1024
        ),
    )(
        key_value_weight.transpose(1, 2, 0).reshape(HEAD_WIDTH, width),
        hidden,
        norm_gain,
        key_value_bias,
        stored_page_pool,
        page_request,
        prefix_len,
        queries,
        new_key_value,
        jnp.asarray(cosine),
        jnp.asarray(sine),
    )


def solution(mesh):
    shape = dict(mesh.shape)
    small = shape["pool"] == 8 and shape["groups"] == 2 and shape["tensor"] == 2
    return jax.shard_map(
        fused if small else local,
        mesh=mesh,
        in_specs=(
            P(("groups", "pool"), "tensor"),
            P("tensor"),
            P("tensor", None, "pool"),
            P(None, "tensor"),
            P(("groups", "pool"), None, None, "tensor"),
            P(("groups", "pool")),
            P(("groups", "pool")),
            P(("groups", "pool"), "tensor"),
            P(("groups", "pool"), None, "tensor"),
        ),
        out_specs=P(("groups", "pool"), "tensor"),
        check_vma=False,
    )
```

```python
import functools
import math

import numpy as np
import jax
import jax.numpy as jnp
from jax import lax
from jax.experimental import pallas as pl
from jax.experimental.pallas import tpu as pltpu
from jax.sharding import PartitionSpec as P

MODEL_WIDTH = 8192
HEADS_PER_GROUP = 8
HEAD_WIDTH = 128
CAP = 1


rope_base = 1000000.0
epsilon = 1e-06
MESH = pl.DeviceIdType.MESH


def apply_rotation(key_portion, token_positions):
    half_dim = key_portion.shape[-1] // 2
    frequency = rope_base ** (
        -(jnp.arange(half_dim, dtype=jnp.float32) * 2.0 / key_portion.shape[-1])
    )
    angles = token_positions.astype(jnp.float32)[:, None] * frequency[None, :]
    cosine = jnp.cos(angles)[:, None, :]
    sine_part = jnp.sin(angles)[:, None, :]
    lead_half = key_portion[..., :half_dim]
    tail_half = key_portion[..., half_dim:]
    return jnp.concatenate(
        [lead_half * cosine - tail_half * sine_part, tail_half * cosine + lead_half * sine_part],
        axis=-1,
    )


def absorb(running, query_heads, key_portion, value_part, visible):
    highest, mass_sum, weighted = running
    scores = jnp.einsum(
        "hgqd,khd->hgqk", query_heads, key_portion, preferred_element_type=jnp.float32
    ) * query_heads.shape[-1] ** (-0.5)
    scores = jnp.where(visible, scores, -jnp.inf)
    new_high = jnp.maximum(highest, jnp.max(scores, axis=-1))
    anchor = jnp.where(jnp.isfinite(new_high), new_high, 0.0)
    prob_rows = jnp.exp(scores - anchor[..., None])
    factor = jnp.exp(highest - anchor)
    mass_sum = mass_sum * factor + jnp.sum(prob_rows, axis=-1)
    weighted = weighted * factor[..., None] + jnp.einsum(
        "hgqk,khd->hgqd",
        prob_rows.astype(jnp.bfloat16),
        value_part,
        preferred_element_type=jnp.float32,
    )
    return (new_high, mass_sum, weighted)


def local(
    hidden,
    norm_gain,
    key_value_weight,
    key_value_bias,
    stored_page_pool,
    page_request,
    prefix_len,
    queries,
    new_key_value,
):
    row_count = hidden.shape[0]
    wide_hidden = hidden.astype(jnp.float32)
    scaled_scores = (wide_hidden * norm_gain.astype(jnp.float32)[None, :]).astype(jnp.bfloat16)
    local_squares = jnp.sum(wide_hidden * wide_hidden, axis=1)
    piece = lax.all_gather(key_value_weight, "pool", axis=2, tiled=True)
    width_part = piece.shape[2]
    product = jnp.dot(
        scaled_scores,
        piece.reshape(piece.shape[0], 2 * width_part),
        preferred_element_type=jnp.float32,
    )
    partial_value = product.reshape(row_count, 2, width_part)
    squares = lax.psum(local_squares, "tensor")
    projected_hidden = lax.psum_scatter(
        partial_value.astype(jnp.bfloat16), "tensor", scatter_dimension=2, tiled=True
    ).astype(jnp.float32)
    inverse_frequency = lax.rsqrt(squares / MODEL_WIDTH + epsilon)
    local_heads = projected_hidden.shape[2] // HEAD_WIDTH
    kv_rows = (
        inverse_frequency[:, None, None] * projected_hidden
        + key_value_bias.astype(jnp.float32)[None]
    )
    kv_rows = kv_rows.reshape(row_count, 2, local_heads, HEAD_WIDTH)
    token_positions = jnp.arange(row_count, dtype=jnp.int32)
    restored_prefix_keys = apply_rotation(kv_rows[:, 0], token_positions).astype(jnp.bfloat16)
    restored_prefix_values = kv_rows[:, 1].astype(jnp.bfloat16)
    fresh_count = queries.shape[0]
    query_heads = queries.reshape(fresh_count, local_heads, HEADS_PER_GROUP, HEAD_WIDTH).transpose(
        1, 2, 0, 3
    )
    fresh_keys = new_key_value[:, 0].reshape(fresh_count, local_heads, HEAD_WIDTH)
    fresh_values = new_key_value[:, 1].reshape(fresh_count, local_heads, HEAD_WIDTH)
    prefix_ok = token_positions < prefix_len[0]
    causal = jnp.arange(fresh_count)[None, :] <= jnp.arange(fresh_count)[:, None]
    visible = jnp.concatenate(
        [jnp.broadcast_to(prefix_ok[None, :], (fresh_count, row_count)), causal], axis=1
    )
    start_state = (
        jnp.full((local_heads, HEADS_PER_GROUP, fresh_count), -jnp.inf, jnp.float32),
        jnp.zeros((local_heads, HEADS_PER_GROUP, fresh_count), jnp.float32),
        jnp.zeros((local_heads, HEADS_PER_GROUP, fresh_count, HEAD_WIDTH), jnp.float32),
    )
    running = absorb(
        start_state,
        query_heads,
        jnp.concatenate([restored_prefix_keys, fresh_keys], axis=0),
        jnp.concatenate([restored_prefix_values, fresh_values], axis=0),
        visible,
    )
    page_count = page_request.shape[0]
    page_index = jnp.arange(page_count)
    same_request = (page_request[:, None] == page_request[None, :]) & (
        page_index[None, :] < page_index[:, None]
    )
    slot_rank = jnp.sum(same_request.astype(jnp.int32), axis=1)
    pool_size = lax.axis_size("pool")
    page_len = stored_page_pool.shape[1]
    outgoing = (
        jnp.zeros((pool_size, CAP) + stored_page_pool.shape[1:], jnp.bfloat16)
        .at[page_request, slot_rank]
        .set(stored_page_pool)
    )
    occupied = jnp.zeros((pool_size, CAP), jnp.bfloat16).at[page_request, slot_rank].set(1.0)
    arrived, present = (
        lax.all_to_all(outgoing, "pool", split_axis=0, concat_axis=0, tiled=True),
        lax.all_to_all(occupied, "pool", split_axis=0, concat_axis=0, tiled=True),
    )
    slot_total_count = pool_size * CAP
    per_block = math.gcd(slot_total_count, max(1, 1024 // page_len))
    grouped = arrived.reshape(
        slot_total_count // per_block, per_block * page_len, 2, local_heads, HEAD_WIDTH
    )
    live_keys = (
        jnp.repeat(present.reshape(slot_total_count // per_block, per_block), page_len, axis=1)
        > 0.5
    )

    def visit_block(carried, scan_item):
        page_block, is_live = scan_item
        return (
            absorb(carried, query_heads, page_block[:, 0], page_block[:, 1], is_live[None, :]),
            None,
        )

    running, unused = lax.scan(visit_block, running, (grouped, live_keys))
    highest, mass_sum, weighted = running
    attended = weighted / mass_sum[..., None]
    return attended.transpose(2, 0, 1, 3).reshape(fresh_count, -1).astype(jnp.bfloat16)


PIECES = 8
ALONG_Z = 4
ALONG_Y = 4
PLANE_Y = 6
REST_AT = 13
PAGES_AT = 13
EARLY = 2
AT_ONCE = (2, 2, 99, 3)
MASKED = -1e30
FLAG_ROWS = 16


def rotation_tables(row_count):
    half = HEAD_WIDTH // 2
    frequency = rope_base ** (-(np.arange(half, dtype=np.float64) * 2.0 / HEAD_WIDTH))
    angles = np.arange(row_count, dtype=np.float64)[:, None] * frequency[None, :]
    cosine, sine = np.cos(angles), np.sin(angles)
    return (
        np.concatenate([cosine, cosine], axis=1).astype(np.float32),
        np.concatenate([-sine, sine], axis=1).astype(np.float32),
    )


def fused_kernel(
    w_ref, h_ref, gain_ref, bias_ref, page_ref, req_ref, plen_ref, q_ref, nkv_ref, cos_ref, sin_ref,
    out_ref,
    wbuf, hraw, hs, accs, psend_buf, precv_buf, ss_send, ss_recv, pout, pin, qbuf, kbuf, vbuf, obuf,
    m_st, l_st, a_st, flat_pages,
    h_sem, own_sem, page_self_sem, w_send, w_recv, part_send, part_recv, ss_sems, pg_send, pg_recv,
):
    f32, bf16 = jnp.float32, jnp.bfloat16
    rows, sub = hs.shape[1], hs.shape[2]
    x = lax.axis_index("groups")
    me = lax.axis_index("pool")
    t = lax.axis_index("tensor")
    z, y = me // 2, lax.rem(me, 2)
    ox, oy, ot = 1 - x, 1 - y, 1 - t
    depth = 4

    def device(g, p, c):
        return {"groups": g, "pool": p, "tensor": c}

    x_peer = device(ox, me, t)
    y_peer = device(x, z * 2 + oy, t)
    low = z < depth // 2
    inside = (z > 0) & (z < depth - 1)
    up, down = jnp.minimum(z + 1, depth - 1), jnp.maximum(z - 1, 0)
    far_peer = device(x, jnp.where(low, up, down) * 2 + y, t)
    near_peer = device(x, jnp.where(low, down, up) * 2 + y, t)
    t_peer = device(x, me, ot)

    blocks = h_sem.shape[0]
    block_rows = rows // blocks

    def hidden_copy(b):
        window = pl.ds(b * block_rows, block_rows)
        return pltpu.make_async_copy(h_ref.at[window], hraw.at[window], h_sem.at[b])

    for b in range(blocks):
        hidden_copy(b).start()
    own_copies = [
        pltpu.make_async_copy(w_ref.at[:, pl.ds(i * sub, sub)], wbuf.at[me, i], own_sem.at[i])
        for i in range(PIECES)
    ]
    for copy in own_copies:
        copy.start()

    barrier = pltpu.get_barrier_semaphore()
    for o in range(1, 8):
        pl.semaphore_signal(
            barrier, inc=1, device_id=device(x, lax.rem(me + o, 8), t), device_id_type=MESH
        )
    pl.semaphore_signal(barrier, inc=1, device_id=x_peer, device_id_type=MESH)
    pl.semaphore_signal(barrier, inc=1, device_id=t_peer, device_id_type=MESH)
    page_len = page_ref.shape[1]
    heads = 2
    width = heads * HEAD_WIDTH

    gain = gain_ref[...].astype(f32).reshape(1, PIECES * sub)

    step_rows = 16

    def scale_block(b):
        hidden_copy(b).wait()

        @pl.loop(0, block_rows // step_rows)
        def _(i):
            at = pl.ds(pl.multiple_of(b * block_rows + i * step_rows, step_rows), step_rows)
            wide = hraw[at, :].astype(f32)
            scaled = (wide * gain).astype(bf16)
            for i in range(PIECES):
                hs[i, at, :] = scaled[:, i * sub : (i + 1) * sub]
            total = jnp.sum(wide * wide, axis=1, keepdims=True)
            ss_send[at, :] = jnp.broadcast_to(total, (step_rows, HEAD_WIDTH))

    fresh = q_ref.shape[0]
    group_rows = HEADS_PER_GROUP * fresh
    scale = HEAD_WIDTH ** (-0.5)
    for j in range(heads):
        for g in range(HEADS_PER_GROUP):
            at = (j * HEADS_PER_GROUP + g) * HEAD_WIDTH
            qbuf[j, g * fresh : (g + 1) * fresh, :] = q_ref[:, at : at + HEAD_WIDTH]

    def inner(a, b):
        return lax.dot_general(a, b, (((1,), (1,)), ((), ())), preferred_element_type=f32)

    def absorb(j, scores, values, first=False):
        high = jnp.max(scores, axis=1, keepdims=True)
        if not first:
            before = m_st[j][:, :1]
            high = jnp.maximum(before, high)
        weights = jnp.exp(scores - high)
        mass = jnp.broadcast_to(jnp.sum(weights, axis=1, keepdims=True), (group_rows, HEAD_WIDTH))
        total = jnp.dot(weights.astype(bf16), values, preferred_element_type=f32)
        if not first:
            factor = jnp.exp(before - high)
            mass = mass + l_st[j] * factor
            total = total + a_st[j] * factor
        m_st[j] = jnp.broadcast_to(high, (group_rows, HEAD_WIDTH))
        l_st[j] = mass
        a_st[j] = total

    fresh_wide = nkv_ref[...].astype(f32)
    new_keys, new_values = fresh_wide[:, 0, :].astype(bf16), fresh_wide[:, 1, :].astype(bf16)
    for j in range(heads):
        kc = j * HEAD_WIDTH
        near = inner(qbuf[j], new_keys[:, kc : kc + HEAD_WIDTH]) * scale
        row_at = lax.rem(lax.broadcasted_iota(jnp.int32, near.shape, 0), fresh)
        near = jnp.where(lax.broadcasted_iota(jnp.int32, near.shape, 1) <= row_at, near, MASKED)
        absorb(j, near, new_values[:, kc : kc + HEAD_WIDTH], True)

    for b in range(EARLY):
        scale_block(b)
    pl.semaphore_wait(barrier, 9)

    def nth(r):
        return jnp.where(x == 0, r, PIECES - 1 - r)

    def copy_of(way, slot, r, peer):
        piece = nth(r)
        return pltpu.make_async_remote_copy(
            src_ref=wbuf.at[slot, piece],
            dst_ref=wbuf.at[slot, piece],
            send_sem=w_send.at[way, slot, piece],
            recv_sem=w_recv.at[slot, piece],
            device_id=peer,
            device_id_type=MESH,
        )

    in_flight = [[] for _ in AT_ONCE]

    def run_if(cond, do):
        if cond is None:
            do()
        else:
            pl.when(cond)(do)

    def send(way, slot, r, peer, cond=None):
        queue = in_flight[way]
        if len(queue) >= AT_ONCE[way]:
            before, earlier = queue.pop(0)
            run_if(before, earlier.wait_send)
        copy = copy_of(way, slot, r, peer)
        queue.append((cond, copy))
        run_if(cond, copy.start)

    def arrive(slot, r):
        copy_of(2, slot, r, x_peer).wait_recv()

    for copy in own_copies:
        copy.wait()
    def send_own(r):
        send(1, me, r, near_peer, inside)
        send(0, me, r, far_peer)

    for r in range(2):
        send_own(r)
        if r < PIECES - PLANE_Y:
            send(3, me, r, y_peer)

    mirrored = jnp.where(low, z, depth - 1 - z)

    def plane(k):
        o = 1 - mirrored if k == 0 else k + 1
        return jnp.where(low, o, depth - 1 - o)

    here_y, there_y = lambda k: plane(k) * 2 + y, lambda k: plane(k) * 2 + oy
    plane_y = z * 2 + oy

    def on_z(k, r):
        slot = here_y(k)
        arrive(slot, r)
        if k > 0:
            send(1, slot, r, near_peer, inside)
        if r < ALONG_Y:
            send(3, slot, r, y_peer)
        if r < PIECES - ALONG_Z:
            send(2, slot, r, x_peer)
        if k == 0 and r + 2 < ALONG_Z:
            send_own(r + 2)
        if k == 1:
            send(0, here_y(0), r, far_peer, inside)

    def on_y(k, r):
        slot = there_y(k)
        arrive(slot, r)
        send(2, slot, r, x_peer)

    def on_plane(r):
        arrive(plane_y, r)
        send(2, plane_y, r, x_peer)

    def multiply(p, pieces, first):
        @pl.loop(0, rows // 256)
        def _(b):
            at = pl.ds(pl.multiple_of(b * 256, 256), 256)
            total = None if first else accs[p, at, :]
            for r in pieces:
                shards = wbuf[pl.ds(p * 2, 2), nth(r)].reshape(2 * HEAD_WIDTH, sub)
                part = lax.dot_general(
                    hs[nth(r), at, :], shards, (((1,), (1,)), ((), ())), preferred_element_type=f32
                )
                total = part if total is None else total + part
            accs[p, at, :] = total

    def part_copy(p):
        at = lax.rem(p, 2)
        return pltpu.make_async_remote_copy(
            src_ref=psend_buf.at[at],
            dst_ref=precv_buf.at[at],
            send_sem=part_send.at[at],
            recv_sem=part_recv.at[at],
            device_id=t_peer,
            device_id_type=MESH,
        )

    def complete(p):
        @pl.when(p // 2 != t)
        def _():
            psend_buf[lax.rem(p, 2)] = accs[p].astype(bf16)
            part_copy(p).start()


    def pack(d):
        taken = [(req_ref[i] == d).astype(f32) for i in range(page_ref.shape[0])]
        picks = [(jnp.zeros((32, 2 * width), f32) + one).astype(bf16) for one in taken]
        for c in range(0, page_len, 32):
            total = flat_pages[0, c : c + 32, :] * picks[0]
            for i in range(1, page_ref.shape[0]):
                total = total + flat_pages[i, c : c + 32, :] * picks[i]
            pout[d, c : c + 32, :] = total
        flag = sum(taken[1:], taken[0])
        pout[d, page_len:, :] = (jnp.full((FLAG_ROWS, pout.shape[2]), 1.0, f32) * flag).astype(bf16)

    def page_copy(o, source, target):
        return pltpu.make_async_remote_copy(
            src_ref=pout.at[target],
            dst_ref=pin.at[source],
            send_sem=pg_send.at[o],
            recv_sem=pg_recv.at[o],
            device_id=device(x, target, t),
            device_id_type=MESH,
        )

    self_page = pltpu.make_async_copy(pout.at[me], pin.at[me], page_self_sem)
    page_sends = [page_copy(o, me, lax.rem(me + o, 8)) for o in range(1, 8)]
    ss_copy = pltpu.make_async_remote_copy(
        src_ref=ss_send,
        dst_ref=ss_recv,
        send_sem=ss_sems.at[0],
        recv_sem=ss_sems.at[1],
        device_id=t_peer,
        device_id_type=MESH,
    )

    def flatten(i):
            for c in range(0, page_len, 32):
                wide = page_ref[i, c : c + 32].astype(f32)
                flat_pages[i, c : c + 32, :width] = wide[:, 0, :].astype(bf16)
                flat_pages[i, c : c + 32, width:] = wide[:, 1, :].astype(bf16)

    def send_pages():
        self_page.start()
        for copy in page_sends:
            copy.start()

    def rest_of_plane():
        for r in range(PIECES - PLANE_Y, PLANE_Y):
            send(3, me, r, y_peer)

    def norms():
        ss_copy.wait()

        @pl.loop(0, rows // 128)
        def _(r):
            at = pl.ds(pl.multiple_of(r * 128, 128), 128)
            ss_send[at, :] = lax.rsqrt((ss_send[at, :] + ss_recv[at, :]) / MODEL_WIDTH + epsilon)

    beside = {}

    def then(n, *work):
        beside.setdefault(n, []).extend(work)

    for b in range(EARLY, blocks):
        then(b - EARLY, functools.partial(scale_block, b))
    for i in range(page_ref.shape[0]):
        then(i, functools.partial(flatten, i))
    for d in range(8):
        then(4 + d // 2, functools.partial(pack, d))
    then(blocks - EARLY, ss_copy.start)
    then(REST_AT, rest_of_plane)
    then(PAGES_AT, send_pages)
    for i in range(4):
        then(8 + i, functools.partial(multiply, plane(0), (i,), i == 0))
        then(12 + i, functools.partial(multiply, plane(1), (i,), i == 0))
    then(14, norms)
    then(16, functools.partial(multiply, plane(2), (0, 1), True))
    then(17, functools.partial(multiply, plane(2), (2, 3), False))

    for r in range(PIECES - PLANE_Y):
        on_plane(r)
    lag = 2
    for n in range(18):
        if n < 3 * ALONG_Z:
            on_z(n // ALONG_Z, n % ALONG_Z)
        k, r = (n - lag) // ALONG_Z, (n - lag) % ALONG_Z
        if n >= lag and k < 3 and r < ALONG_Y:
            on_y(k, r)
        for work in beside.get(n, []):
            work()

    def pages_in():
        self_page.wait()
        for o in range(1, 8):
            page_copy(o, lax.rem(me + 8 - o, 8), me).wait_recv()
        flags = jnp.concatenate(
            [pin[i, page_len:, :HEAD_WIDTH].astype(f32)[:1, :] for i in range(8)], axis=1
        )
        for j in range(heads):
            kc, vc = j * HEAD_WIDTH, (heads + j) * HEAD_WIDTH
            keys = pin[:, :page_len, kc : kc + HEAD_WIDTH].reshape(8 * page_len, HEAD_WIDTH)
            values = pin[:, :page_len, vc : vc + HEAD_WIDTH].reshape(8 * page_len, HEAD_WIDTH)
            absorb(j, jnp.where(flags > 0.5, inner(qbuf[j], keys) * scale, MASKED), values)

    half = HEAD_WIDTH // 2

    def finish(j):
        p = 2 * t + j
        part_copy(p).wait_recv()
        bias = jnp.where(j == 0, bias_ref[:, :HEAD_WIDTH].astype(f32), bias_ref[:, HEAD_WIDTH:].astype(f32))

        @pl.loop(0, rows // 128)
        def _(r):
            at = pl.ds(pl.multiple_of(r * 128, 128), 128)
            both = accs[p, at, :] + precv_buf[j, at, :].astype(f32)
            lead, tail = both[:, :HEAD_WIDTH], both[:, HEAD_WIDTH:]
            inverse = ss_send[at, :]
            key = jnp.concatenate([lead[:, :half], tail[:, :half]], axis=1) * inverse + bias[0:1]
            value = jnp.concatenate([lead[:, half:], tail[:, half:]], axis=1) * inverse + bias[1:2]
            turned = jnp.concatenate([key[:, half:], key[:, :half]], axis=1)
            kbuf[at, :] = (key * cos_ref[at, :] + turned * sin_ref[at, :]).astype(bf16)
            vbuf[at, :] = value.astype(bf16)

        scores = inner(qbuf[j], kbuf[...]) * scale
        seen = lax.broadcasted_iota(jnp.int32, scores.shape, 1) < plen_ref[0]
        absorb(j, jnp.where(seen, scores, MASKED), vbuf[...])

    def await_x(slot, first):
        for r in range(PIECES - 1, first - 1, -1):
            arrive(slot, r)

    def close(k):
        await_x(here_y(k), ALONG_Z)
        await_x(there_y(k), ALONG_Y)
        multiply(plane(k), range(ALONG_Y, PIECES), False)
        complete(plane(k))

    for r in range(PIECES - PLANE_Y, PLANE_Y):
        arrive(plane_y, r)
    multiply(z, range(PLANE_Y), True)
    await_x(plane_y, PLANE_Y)
    multiply(z, range(PLANE_Y, PIECES), False)
    complete(z)
    close(0)
    close(1)
    finish(jnp.where(low, 0, 1))
    pages_in()
    close(2)
    finish(jnp.where(low, 1, 0))

    for j in range(heads):
        obuf[j] = (a_st[j] / l_st[j]).astype(bf16)
    for j in range(heads):
        for g in range(HEADS_PER_GROUP):
            at = (j * HEADS_PER_GROUP + g) * HEAD_WIDTH
            out_ref[:, at : at + HEAD_WIDTH] = obuf[j, g * fresh : (g + 1) * fresh, :]

    for queue in in_flight:
        for cond, copy in queue:
            run_if(cond, copy.wait_send)
    for copy in page_sends:
        copy.wait_send()
    for i in range(2):
        part_copy(2 * ot + i).wait_send()


def fused(
    hidden, norm_gain, key_value_weight, key_value_bias, stored_page_pool, page_request, prefix_len,
    queries, new_key_value,
):
    rows, width = hidden.shape
    fresh = queries.shape[0]
    pages, page_len = stored_page_pool.shape[:2]
    cosine, sine = rotation_tables(rows)
    vmem = pl.BlockSpec(memory_space=pltpu.VMEM)
    smem = pl.BlockSpec(memory_space=pltpu.SMEM)
    anywhere = pl.BlockSpec(memory_space=pl.ANY)
    bf16, f32 = jnp.bfloat16, jnp.float32
    dma = pltpu.SemaphoreType.DMA
    return pl.pallas_call(
        fused_kernel,
        out_shape=jax.ShapeDtypeStruct(queries.shape, bf16),
        in_specs=[anywhere, anywhere, vmem, vmem, vmem, smem, smem, vmem, vmem, vmem, vmem],
        out_specs=vmem,
        scratch_shapes=[
            pltpu.VMEM((8, PIECES, HEAD_WIDTH, width // PIECES), bf16),
            pltpu.VMEM((rows, width), bf16),
            pltpu.VMEM((PIECES, rows, width // PIECES), bf16),
            pltpu.VMEM((4, rows, 2 * HEAD_WIDTH), f32),
            pltpu.VMEM((2, rows, 2 * HEAD_WIDTH), bf16),
            pltpu.VMEM((2, rows, 2 * HEAD_WIDTH), bf16),
            pltpu.VMEM((rows, HEAD_WIDTH), f32),
            pltpu.VMEM((rows, HEAD_WIDTH), f32),
            pltpu.VMEM((8, page_len + FLAG_ROWS, 4 * HEAD_WIDTH), bf16),
            pltpu.VMEM((8, page_len + FLAG_ROWS, 4 * HEAD_WIDTH), bf16),
            pltpu.VMEM((2, HEADS_PER_GROUP * fresh, HEAD_WIDTH), bf16),
            pltpu.VMEM((rows, HEAD_WIDTH), bf16),
            pltpu.VMEM((rows, HEAD_WIDTH), bf16),
            pltpu.VMEM((2, HEADS_PER_GROUP * fresh, HEAD_WIDTH), bf16),
            pltpu.VMEM((2, HEADS_PER_GROUP * fresh, HEAD_WIDTH), f32),
            pltpu.VMEM((2, HEADS_PER_GROUP * fresh, HEAD_WIDTH), f32),
            pltpu.VMEM((2, HEADS_PER_GROUP * fresh, HEAD_WIDTH), f32),
            pltpu.VMEM((pages, page_len, 4 * HEAD_WIDTH), bf16),
            dma((8,)), dma((PIECES,)), dma,
            dma((4, 8, PIECES)), dma((8, PIECES)),
            dma((2,)), dma((2,)), dma((2,)), dma((8,)), dma((8,)),
        ],
        compiler_params=pltpu.CompilerParams(
            collective_id=0, has_side_effects=True, vmem_limit_bytes=56 * 1024 * 1024
        ),
    )(
        key_value_weight.transpose(1, 2, 0).reshape(HEAD_WIDTH, width),
        hidden,
        norm_gain,
        key_value_bias,
        stored_page_pool,
        page_request,
        prefix_len,
        queries,
        new_key_value,
        jnp.asarray(cosine),
        jnp.asarray(sine),
    )


def solution(mesh):
    shape = dict(mesh.shape)
    small = shape["pool"] == 8 and shape["groups"] == 2 and shape["tensor"] == 2
    return jax.shard_map(
        fused if small else local,
        mesh=mesh,
        in_specs=(
            P(("groups", "pool"), "tensor"),
            P("tensor"),
            P("tensor", None, "pool"),
            P(None, "tensor"),
            P(("groups", "pool"), None, None, "tensor"),
            P(("groups", "pool")),
            P(("groups", "pool")),
            P(("groups", "pool"), "tensor"),
            P(("groups", "pool"), None, "tensor"),
        ),
        out_specs=P(("groups", "pool"), "tensor"),
        check_vma=False,
    )
```
